1024 devices in a mesh: dom: 8 (over y), map: 8 (over z), slab: 16 (over x, core).
Axes of the slice: x: 8, y: 8, z: 8, core: 2. Of those that a mesh axis runs over, the one named last changes fastest.
Arguments:
- particles: bfloat16 [256, 64, 4096], P(('dom', 'map'), 'slab'), may hold values from -6 to 6
- class_list: int32 [256, 2], P(('dom', 'map')), may hold values from 0 to 7, all different within a row; in each aligned block of 4 rows (0 to 3, 4 to 7, ...) at most 2 rows name the same one
- orient: int32 [256, 2], P(('dom', 'map')), may hold values from 0 to 3
- ctf_index: int32 [256], P(('dom', 'map')), may hold values from 0 to 63
- tomo_id: int32 [256], P(('dom', 'map')), may hold values from 0 to 31, as said below
- defocus: float32 [64], replicated, may hold values from 20 to 200
- tomo_gain: float32 [32], replicated, may hold values from 0.5 to 2
- maps: float32 [8, 128, 128, 128], P('map', 'slab'), may hold values from -6 to 6
Outputs:
- real_grad: float32 [8, 128, 128, 128], P('map', None, 'slab')
- scores: float32 [256, 2], P(('dom', 'map'))
The draws below stay inside these ranges and needn't reach their ends.
Inputs may be any that keep to these rules, and one draw needn't show every extreme that they name: `class_list`: each particle lists 2 different classes; the particles of one device name no class more than 2 times. `tomo_id`: the particles on dom index d belong to tomograms d * 4 to (d + 1) * 4 - 1.
All inputs are finite; a program needn't handle non-finite values.
Results may differ from the reference program's by a relative error of at most 0.0003.
Values may be sent and summed in bfloat16 or wider, within the bound.
A program may use at most 64 MiB of HBM per device.

```python
import math
import jax
import jax.numpy as jnp
import numpy as np
from jax import lax

L = 128
BOX = 64
K = 2
NCTF = 64
TOMO_DEV = 4
P_DEV = 4
CLS = 8
PARTICLES = 256
TOMOS = 32
CAP = 2
NPC = 64
N_SLAB = 16


def draw_tomo_id(key, part):
    block = PARTICLES * TOMO_DEV // TOMOS
    offsets = jax.random.randint(key, (PARTICLES,), 0, TOMO_DEV).astype(jnp.int32)
    offsets = offsets.at[0].set(0)
    offsets = offsets.at[PARTICLES - 1].set(TOMO_DEV - 1)
    group = jnp.arange(PARTICLES, dtype=jnp.int32) // block
    return (group * TOMO_DEV + offsets).astype(jnp.int32)


def with_ends(drawn, key, smallest, top_value):
    longest = drawn.shape.index(max(drawn.shape))
    spots = []
    for shift in (0, 1):
        where = [jax.random.randint(jax.random.fold_in(key, axis), (), 0, length) for axis, length in enumerate(drawn.shape)]
        where[longest] = (where[longest] + shift) % drawn.shape[longest]
        spots.append(tuple(where))
    return drawn.at[spots[0]].set(smallest).at[spots[1]].set(top_value)


def levels(own_key, extent, split, smallest, top_value):
    level, own = 1.0, jax.random.fold_in(own_key, 6)
    for axis_at, blocks in split:
        draws = jnp.exp(jax.random.uniform(jax.random.fold_in(own, axis_at), (blocks,), jnp.float32, smallest / len(split), top_value / len(split)))
        level = level * jnp.repeat(draws, extent[axis_at] // blocks).reshape([-1 if axis == axis_at else 1 for axis in range(len(extent))])
    return level


def shared_out(rng, own, number, rows, number_of, top, bound, slope):
    order = jax.random.permutation(rng, number_of)
    crowded, usual = portions_of(number_of, rows * top, bound, slope, True), portions_of(number_of, rows * top, bound, slope, False)
    places = jnp.arange(number_of)

    def named(tallies, turn):
        used = int((tallies > 0).sum())
        fixed = max(1, used // 4)
        moved = fixed + (places - fixed + turn * (used - fixed)) % max(1, number_of - fixed)
        return jnp.zeros((number_of,), jnp.int32).at[order[jnp.where(places < fixed, places, moved)]].set(jnp.asarray(tallies, jnp.int32))

    tallies = jnp.where(number % 4 == 0, named(crowded, number // 4), named(usual, number - number // 4 - 1))
    mixed = jax.random.permutation(jax.random.fold_in(own, 3), number_of)
    source_of, sink = mixed[0:number_of // 2 * 2:2], mixed[1:number_of // 2 * 2:2]
    margin = jnp.minimum(tallies[source_of] - 1, bound - tallies[sink]) // 2
    margin = jnp.where((source_of == order[0]) | (sink == order[0]) | (tallies[sink] == 0), 0, jnp.maximum(margin, 0))
    moved = jax.random.randint(jax.random.fold_in(own, 4), (number_of // 2,), 0, 1 << 20) % (margin + 1)
    tallies = tallies.at[source_of].add(-moved).at[sink].add(moved)
    members = jnp.searchsorted(jnp.cumsum(tallies), jnp.arange(rows * top), side="right").astype(jnp.int32)
    table = members.reshape(top, rows).T
    table = table[jax.random.permutation(jax.random.fold_in(own, 1), rows)]
    turn = jax.random.randint(jax.random.fold_in(own, 2), (rows, 1), 0, top)
    return jnp.take_along_axis(table, (jnp.arange(top)[None, :] + turn) % top, axis=1)


def portions_of(number_of, total, most, lean, full):
    portions = [(1 << 20) // math.isqrt(rank ** lean) + 1 for rank in range(1, number_of + 1)]
    largest = most if full else min(most, max(-(-total // number_of), total * portions[0] // sum(portions)))
    least = 1 if total - largest >= number_of - 1 else 0
    given, spare = [largest] + [least] * (number_of - 1), total - largest - least * (number_of - 1)
    while spare > 0:
        movable = [i for i in range(1, number_of) if given[i] < largest] or [i for i in range(1, number_of) if given[i] < most]
        whole, budget = sum([portions[i] for i in movable]), spare
        for i in movable:
            extra = min(most - given[i], max(1, budget * portions[i] // whole), spare)
            given[i] = given[i] + extra
            spare = spare - extra
    return np.array(given)


def scatter_about(rng, dims, deviation, most, pieces=(), kind=jnp.bfloat16):
    loudness = levels(rng, dims, pieces, -0.22, 0.18) if pieces else 1.0
    values = jax.random.normal(rng, dims, jnp.float32) * deviation * loudness
    return jnp.minimum(jnp.maximum(values, -most), most).astype(kind)


def setup_inputs(seed: int = 0) -> dict:
    splits = jax.random.split(jax.random.key(seed), 9)
    particles = scatter_about(splits[0], (PARTICLES, BOX, BOX * BOX), 1.0, 6.0, ((0, 64), (1, 16)))
    class_list_keys = jax.random.split(jax.random.fold_in(splits[1], 1), PARTICLES // P_DEV)
    class_list_turns = jax.random.permutation(jax.random.fold_in(splits[1], 3), PARTICLES // P_DEV)
    class_list = jax.vmap(lambda own, number: shared_out(jax.random.fold_in(splits[1], 2), own, number, P_DEV, CLS, K, CAP, 2))(class_list_keys, class_list_turns).reshape((PARTICLES, K))
    orient = with_ends(jax.random.randint(splits[2], (PARTICLES, K), 0, 4), jax.random.fold_in(splits[2], 1), 0, 3).astype(jnp.int32)
    ctf_index = with_ends(jax.random.randint(splits[3], (PARTICLES,), 0, NCTF), jax.random.fold_in(splits[3], 1), 0, NCTF - 1).astype(jnp.int32)
    tomo_id = draw_tomo_id(jax.random.fold_in(splits[8], 71), 0)
    defocus = jnp.clip(jnp.exp(jax.random.uniform(splits[5], (NCTF,), jnp.float32, math.log(20.0), math.log(200.0))), 20.0, 200.0)
    tomo_gain = jnp.clip(jnp.exp(jax.random.uniform(splits[6], (TOMOS,), jnp.float32, math.log(0.5), math.log(2.0))), 0.5, 2.0)
    maps = scatter_about(splits[7], (CLS, L, L, L), 1.0, 6.0, ((0, 8), (1, 16)), jnp.float32)
    return {"particles": particles, "class_list": class_list, "orient": orient, "ctf_index": ctf_index, "tomo_id": tomo_id, "defocus": defocus, "tomo_gain": tomo_gain, "maps": maps}


TAU_REG = 0.1
PHASE_SHIFT = 0.1

def wrap_freq(index, grid_size):
    return jnp.where(index < grid_size // 2, index, index - grid_size)

def cas_table(freqs, grid_size):
    points = jnp.arange(grid_size, dtype=jnp.int32)
    phase = freqs[:, None] * points[None, :] % grid_size
    angle = phase.astype(jnp.float32) * (2.0 * math.pi / grid_size)
    return (jnp.cos(angle) + jnp.sin(angle)) / math.sqrt(grid_size)

def plane_freqs(total, box_size, planes):
    index = jnp.arange(total, dtype=jnp.int32)
    device = index // (2 * planes)
    offset = index % (2 * planes)
    low_freq = wrap_freq(device * planes + offset, box_size)
    high_freq = box_size // 2 + device * planes + offset - planes
    return jnp.where(offset < planes, low_freq, high_freq)

def rotation_table(box_size):
    rows = jnp.arange(box_size, dtype=jnp.int32)[:, None]
    cols = jnp.arange(box_size, dtype=jnp.int32)[None, :]
    neg_rows = -rows % box_size
    neg_cols = -cols % box_size
    turns = [rows * box_size + cols, cols * box_size + neg_rows, neg_rows * box_size + neg_cols, neg_cols * box_size + rows]
    return jnp.stack([jnp.broadcast_to(turn, (box_size, box_size)).reshape(-1) for turn in turns])

def square_freqs(box_size, first, planes):
    plane_f = wrap_freq(first + jnp.arange(planes, dtype=jnp.int32), box_size)
    inner = wrap_freq(jnp.arange(box_size, dtype=jnp.int32), box_size)
    total = plane_f[:, None, None] ** 2 + inner[None, :, None] ** 2 + inner[None, None, :] ** 2
    return (total.astype(jnp.float32) / float(box_size * box_size)).reshape(planes, box_size * box_size)

def reference(particles, class_list, orient, ctf_index, tomo_id, defocus, tomo_gain, maps):
    half = BOX // 2
    planes = BOX // N_SLAB
    low_index = jnp.arange(BOX, dtype=jnp.int32)
    plane_low = low_index // planes * (2 * planes) + low_index % planes
    window_rows = jnp.concatenate([jnp.arange(half, dtype=jnp.int32), jnp.arange(L - half, L, dtype=jnp.int32)])
    windows = maps[:, plane_low][:, :, window_rows][:, :, :, window_rows].reshape(CLS, BOX, BOX * BOX)
    rotation = rotation_table(BOX)
    squares = square_freqs(BOX, 0, BOX)
    focus_vals = defocus[ctf_index]
    gain_vals = tomo_gain[tomo_id]

    def step(carry, inputs):
        particle, classes, turns, focus, gain = inputs
        contrast = gain * jnp.sin(focus * squares + PHASE_SHIFT)
        values = particle.astype(jnp.float32)
        found = []
        for route in range(K):
            chosen = windows[classes[route]]
            turned = jnp.take(chosen, rotation[turns[route]], axis=1)
            predicted = contrast * turned
            found.append(jnp.sum(values * predicted) / BOX ** 1.5)
            weighted = contrast * (predicted - values)
            back = jnp.take(weighted, rotation[(4 - turns[route]) % 4], axis=1)
            carry = carry.at[classes[route]].add(back)
        return (carry, jnp.stack(found))
    start = jnp.zeros((CLS, BOX, BOX * BOX), jnp.float32)
    sums, scores = lax.scan(step, start, (particles, class_list, orient, focus_vals, gain_vals))
    data_grad = sums * (1.0 / NPC)
    grad = TAU_REG * maps
    grad = grad.at[:, plane_low[:, None, None], window_rows[None, :, None], window_rows[None, None, :]].add(data_grad.reshape(CLS, BOX, BOX, BOX))
    table = cas_table(jnp.arange(L, dtype=jnp.int32), L)
    plane_table = cas_table(plane_freqs(L, BOX, planes), L)

    def transform(block):
        first = jnp.einsum('quv,uy->qyv', block, table, precision=lax.Precision.HIGHEST)
        second = jnp.einsum('qyv,vx->qyx', first, table, precision=lax.Precision.HIGHEST)
        return jnp.einsum('qyx,qz->zyx', second, plane_table, precision=lax.Precision.HIGHEST)
    real_grad = lax.map(transform, grad)
    return (real_grad, scores)
```

```python
import functools
import math

import jax
import jax.numpy as jnp
import numpy as np
from jax import lax
from jax.experimental import pallas as pl
from jax.experimental.pallas import tpu as pltpu
from jax.sharding import PartitionSpec as P

L = 128
BOX = 64
K = 2
P_DEV = 4
PLANES = 4
TAU_REG = 0.1
PHASE_SHIFT = 0.1
F32 = jnp.float32
BF16 = jnp.bfloat16


def ring_order(n):
    order = []
    for step in range(1, n // 2 + 1):
        order += [step] if 2 * step == n else [step, n - step]
    return order


def wrap(index, size):
    return jnp.where(index < size // 2, index, index - size)


def fast_sin(x):
    turns = jnp.floor(x * (1.0 / math.pi) + 0.5)
    r = x - turns * 3.140625
    r = r - turns * 9.67653589793e-4
    odd = turns - 2.0 * jnp.floor(turns * 0.5)
    r = r * (1.0 - 2.0 * odd)
    s = r * r
    poly = -1.0 / 39916800.0
    for c in (1.0 / 362880.0, -1.0 / 5040.0, 1.0 / 120.0, -1.0 / 6.0):
        poly = poly * s + c
    return r + r * s * poly


def split(x):
    high = x.astype(BF16)
    return high, (x - high.astype(F32)).astype(BF16)


def dot(a, b):
    return jnp.dot(a, b, preferred_element_type=F32)


def dot3(a, b):
    return dot(a[0], b[0]) + (dot(a[0], b[1]) + dot(a[1], b[0]))


def tables(n_slab):
    def cas(rows, cols):
        angle = (np.outer(rows, cols) % L) * (2.0 * math.pi / L)
        return (np.cos(angle) + np.sin(angle)) / math.sqrt(L)

    points = np.arange(L)
    wrapped = np.where(np.arange(BOX) < BOX // 2, np.arange(BOX), np.arange(BOX) - BOX)
    rows = cas(points, points)
    window = cas(wrapped, points)
    q = np.arange(2 * PLANES * n_slab)
    s, r = q // (2 * PLANES), q % (2 * PLANES)
    low = s * PLANES + r
    low = np.where(low < BOX // 2, low, low - BOX)
    freq = np.where(r < PLANES, low, BOX // 2 + s * PLANES + r - PLANES)
    planes = cas(points, freq)
    full = np.zeros((L, L))
    full[:, : len(q)] = planes
    picked = np.zeros((L, L))
    half = 2 * n_slab
    for jj in range(2):
        for row in range(half):
            picked[:, jj * half + row] = planes[:, (row // 2) * 2 * PLANES + 2 * (row % 2) + jj]
    none = np.zeros((BOX, L))
    negate = np.zeros((L, L))
    for block in range(2):
        for a in range(BOX):
            negate[block * BOX + a, block * BOX + (-a) % BOX] = 1.0
    first = np.concatenate([window.T, window.T], axis=1) / 64.0
    mats = [
        rows * TAU_REG,
        rows,
        full,
        picked,
        first,
        np.concatenate([window, none]),
        np.concatenate([none, window]),
        negate,
    ]
    pairs = []
    for mat in mats:
        mat = mat.astype(np.float32)
        high = mat.astype(jnp.bfloat16)
        pairs += [high, (mat - high.astype(np.float32)).astype(jnp.bfloat16)]
    return np.stack(pairs)


def kernel(
    sizes,
    part,
    cls,
    ori,
    cidx,
    tid,
    focus,
    gain,
    maps,
    tab,
    out,
    score_out,
    tmp,
    xs,
    send_a,
    recv_a,
    send_m,
    recv_m,
    send1,
    recv1,
    acc,
    wrot,
    ctf,
    sums,
    sc_send,
    sc_recv,
    ss_send,
    ss_recv,
    dbuf,
    rs_recv,
    red,
    dfull,
    send2,
    recv2,
    vbuf,
    m_s,
    m_r,
    a_s,
    a_r,
    c1_s,
    c1_r,
    sc_s,
    sc_r,
    ss_s,
    ss_r,
    rs_s,
    rs_r,
    ag_s,
    ag_r,
    c2_s,
    c2_r,
):
    n_dom, n_map, n_slab = sizes
    rows = L // n_slab
    chunk = L // n_dom
    d, m, s = lax.axis_index("dom"), lax.axis_index("map"), lax.axis_index("slab")
    axes = {"dom": (d, n_dom), "map": (m, n_map), "slab": (s, n_slab)}

    def ahead(axis, step):
        me, n = axes[axis]
        return lax.rem(me + step, n)

    def remote(axis, step, src, dst, ssem, rsem):
        return pltpu.make_async_remote_copy(
            src_ref=src,
            dst_ref=dst,
            send_sem=ssem.at[step],
            recv_sem=rsem.at[step],
            device_id={axis: ahead(axis, step)},
            device_id_type=pl.DeviceIdType.MESH,
        )

    barrier = pltpu.get_barrier_semaphore()
    for axis, (_, n) in axes.items():
        for step in range(1, n):
            pl.semaphore_signal(
                barrier,
                inc=1,
                device_id={axis: ahead(axis, step)},
                device_id_type=pl.DeviceIdType.MESH,
            )

    lane = lax.broadcasted_iota(jnp.int32, (L, L), 1)
    row = lax.broadcasted_iota(jnp.int32, (L, L), 0)
    lane8 = lax.broadcasted_iota(jnp.int32, (8, L), 1)
    row8 = lax.broadcasted_iota(jnp.int32, (8, L), 0)

    for g in range(2):
        both = jnp.concatenate([part[2 * g].astype(F32), part[2 * g + 1].astype(F32)], axis=0)
        up = pltpu.roll(both, 7, 0)
        for k in range(BOX // 2):
            here, above = both[:, k * L : (k + 1) * L], up[:, k * L : (k + 1) * L]
            even = jnp.where(lane8 < BOX, here, pltpu.roll(above, BOX, 1))
            odd = jnp.where(lane8 < BOX, pltpu.roll(here, BOX, 1), above)
            tmp[k] = jnp.where(row8 % 2 == 0, even, pltpu.roll(odd, 1, 0))
        for i in range(4):
            for h in range(2):
                start = (i % 2) * BOX + h
                xs[2 * g + i // 2, pl.ds(start, BOX // 2, stride=2), :] = tmp[:, 2 * i + h, :]

    def build(c, carry):
        found = jnp.int32(0)
        who = [jnp.int32(0)] * 2
        turn = [jnp.int32(0)] * 2
        for p in range(P_DEV):
            for i in range(K):
                hit = cls[i, p] == c
                for k in range(2):
                    mine = jnp.logical_and(hit, found == k)
                    who[k] = jnp.where(mine, p, who[k])
                    turn[k] = jnp.where(mine, ori[i, p], turn[k])
                found = found + hit.astype(jnp.int32)
        meta = jnp.zeros((8, L), F32)
        for k in range(2):
            power = jnp.where(found > k, gain[tid[who[k]]], 0.0)
            meta = jnp.where(row8 == 4 * k, focus[cidx[who[k]]], meta)
            meta = jnp.where(row8 == 4 * k + 1, power, meta)
            meta = jnp.where(row8 == 4 * k + 2, turn[k].astype(F32), meta)
            send_a[c, k * L : (k + 1) * L, :] = xs[who[k]].astype(BF16)
        send_m[c] = meta
        return carry

    lax.fori_loop(0, n_map, build, 0)

    pl.semaphore_wait(barrier, n_dom + n_map + n_slab - 3)

    map_order = ring_order(n_map)
    dom_order = ring_order(n_dom)
    slab_order = ring_order(n_slab)

    def meta_copy(step):
        return remote("map", step, send_m.at[ahead("map", step)], recv_m.at[m], m_s, m_r)

    def data_copy(step):
        return remote("map", step, send_a.at[ahead("map", step)], recv_a.at[m], a_s, a_r)

    for step in map_order:
        meta_copy(step).start()
    for step in map_order:
        data_copy(step).start()

    def table(i):
        return tab[2 * i], tab[2 * i + 1]

    for q in range(2 * PLANES):
        across = dot3(split(maps[0, q]), table(0))
        send1[:, q, :] = dot3(table(1), split(across))

    def first_copy(step):
        return remote(
            "slab",
            step,
            send1.at[pl.ds(ahead("slab", step) * rows, rows)],
            recv1.at[:, pl.ds(s * 2 * PLANES, 2 * PLANES), :],
            c1_s,
            c1_r,
        )

    for step in slab_order:
        first_copy(step).start()
    recv1[:, pl.ds(s * 2 * PLANES, 2 * PLANES), :] = send1[pl.ds(s * rows, rows)]

    negate = tab[14]

    def by_left(x):
        high, low = split(x)
        return dot(negate, high) + dot(negate, low)

    def by_right(x):
        high, low = split(x)
        return dot(high, negate) + dot(low, negate)

    def swapped(x):
        t = x.T
        other = pltpu.roll(pltpu.roll(t, BOX, 0), BOX, 1)
        return jnp.where(row // BOX == lane // BOX, t, other)

    halves = []
    for jp in range(2):
        cut = []
        for jj in range(2):
            plane = maps[0, 2 * jp + jj]
            cut.append(jnp.concatenate([plane[: BOX // 2], plane[L - BOX // 2 :]], axis=0))
        lane64 = lane[:BOX]
        first = jnp.where(lane64 < BOX // 2, cut[0], pltpu.roll(cut[0], BOX, 1))
        second = jnp.where(lane64 < L - BOX // 2, pltpu.roll(cut[1], BOX, 1), cut[1])
        halves.append(jnp.where(lane64 < BOX, first, second))
    window = jnp.concatenate(halves, axis=0)
    window_n = by_right(window)
    wrot[0] = window
    wrot[1] = swapped(window_n)
    wrot[2] = by_left(window_n)
    wrot[3] = swapped(by_left(window))

    fj = wrap(s * PLANES + 2 * (row // BOX) + lane // BOX, BOX)
    fa, fb = wrap(row % BOX, BOX), wrap(lane % BOX, BOX)
    squares = (fj * fj + fa * fa + fb * fb).astype(F32) * (1.0 / (BOX * BOX))

    def contrast(meta, src, total):
        for k in range(2):
            value = meta[4 * k + 1 : 4 * k + 2] * fast_sin(meta[4 * k : 4 * k + 1] * squares + PHASE_SHIFT)
            ctf[src, k] = value
            total = total + value * value
        return total

    power = contrast(send_m[m], m, jnp.zeros((L, L), F32))
    for step in map_order:
        meta_copy(step).wait_recv()
    power = lax.fori_loop(
        1,
        n_map,
        lambda step, total: contrast(recv_m[lax.rem(m + step, n_map)], lax.rem(m + step, n_map), total),
        power,
    )
    dbuf[...] = wrot[0] * power

    sums[...] = jnp.zeros_like(sums)

    def collect(data, meta, src):
        lines = jnp.zeros((8, L), F32)
        for k in range(2):
            z = data[k * L : (k + 1) * L].astype(F32) * ctf[src, k]
            turn = meta[4 * k + 2 : 4 * k + 3]
            found = jnp.zeros((L, L), F32)
            for o in range(4):
                part_o = jnp.where(turn == float(o), z, 0.0)
                sums[o] += part_o
                found = found + part_o * wrot[o]
            lines = jnp.where(row8 == k, jnp.sum(found, axis=0, keepdims=True), lines)
        return lines * (1.0 / BOX**1.5)

    sc_recv[m] = collect(send_a[m], send_m[m], m)
    for step in map_order:
        src = lax.rem(m + n_map - step, n_map)
        remote("map", step, send_a.at[src], recv_a.at[src], a_s, a_r).wait_recv()
        sc_send[src] = collect(recv_a[src], recv_m[src], src)

    def score_copy(step):
        return remote("map", step, sc_send.at[ahead("map", step)], sc_recv.at[m], sc_s, sc_r)

    turned = swapped(by_left(sums[1]) + by_right(sums[3]))
    dbuf[...] = dbuf[...] - (sums[0] + by_left(by_right(sums[2])) + turned)

    def scatter_copy(step):
        return remote("dom", step, dbuf.at[pl.ds(ahead("dom", step) * chunk, chunk)], rs_recv.at[d], rs_s, rs_r)

    for step in dom_order:
        scatter_copy(step).start()
    for step in map_order:
        score_copy(step).start()
    rs_recv[d] = dbuf[pl.ds(d * chunk, chunk)]
    for step in dom_order:
        src = lax.rem(d + n_dom - step, n_dom)
        remote("dom", step, dbuf.at[pl.ds(0, chunk)], rs_recv.at[src], rs_s, rs_r).wait_recv()
    total = rs_recv[0]
    for i in range(1, n_dom):
        total = total + rs_recv[i]
    red[...] = total

    def gather_copy(step):
        return remote("dom", step, red, dfull.at[pl.ds(d * chunk, chunk)], ag_s, ag_r)

    for step in dom_order:
        gather_copy(step).start()
    dfull[pl.ds(d * chunk, chunk)] = total

    for step in map_order:
        src = lax.rem(m + n_map - step, n_map)
        remote("map", step, sc_send.at[src], sc_recv.at[src], sc_s, sc_r).wait_recv()
    flat = [jnp.sum(sc_recv[:, k, :], axis=1, keepdims=True) for k in range(2)]
    lane_m = lax.broadcasted_iota(jnp.int32, (n_map, L), 1)
    ss_send[...] = jnp.where(lane_m == 0, flat[0], jnp.where(lane_m == 1, flat[1], 0.0))

    def spread_copy(step):
        return remote("slab", step, ss_send, ss_recv.at[s], ss_s, ss_r)

    for step in slab_order:
        spread_copy(step).start()
    ss_recv[s] = ss_send[...]

    for step in dom_order:
        src = lax.rem(d + n_dom - step, n_dom)
        remote("dom", step, red, dfull.at[pl.ds(src * chunk, chunk)], ag_s, ag_r).wait_recv()

    for jp in range(2):
        columns = dot3(
            (tab[8][:, :BOX], tab[9][:, :BOX]), split(dfull[jp * BOX : (jp + 1) * BOX])
        )
        send2[:, jp] = columns.reshape(n_slab, rows, L)

    def second_copy(step):
        return remote("slab", step, send2.at[ahead("slab", step)], recv2.at[s], c2_s, c2_r)

    for step in slab_order:
        second_copy(step).start()
    recv2[s] = send2[s]

    for step in slab_order:
        src = lax.rem(s + n_slab - step, n_slab)
        remote(
            "slab",
            step,
            send1.at[pl.ds(0, rows)],
            recv1.at[:, pl.ds(src * 2 * PLANES, 2 * PLANES), :],
            c1_s,
            c1_r,
        ).wait_recv()
    deep = 2 * PLANES * n_slab
    by_plane = (tab[4][:, :deep], tab[5][:, :deep])
    for y in range(rows):
        acc[y] = dot3(by_plane, split(recv1[y]))

    for step in slab_order:
        src = lax.rem(s + n_slab - step, n_slab)
        remote("slab", step, ss_send, ss_recv.at[src], ss_s, ss_r).wait_recv()
    tally = ss_recv[0]
    for i in range(1, n_slab):
        tally = tally + ss_recv[i]
    row_m = lax.broadcasted_iota(jnp.int32, (n_map, L), 0)
    out_row = lax.broadcasted_iota(jnp.int32, (K, P_DEV), 0)
    out_col = lax.broadcasted_iota(jnp.int32, (K, P_DEV), 1)
    found = jnp.zeros((K, P_DEV), F32)
    for p in range(P_DEV):
        for i in range(K):
            c = cls[i, p]
            rank = jnp.int32(0)
            for e in range(p * K + i):
                rank = rank + (cls[e % K, e // K] == c).astype(jnp.int32)
            here = jnp.logical_and(row_m == c, lane_m == rank)
            one = jnp.sum(jnp.where(here, tally, 0.0), axis=0, keepdims=True)
            one = jnp.sum(one, axis=1, keepdims=True)
            found = jnp.where(jnp.logical_and(out_row == i, out_col == p), one, found)
    score_out[...] = found

    for step in slab_order:
        src = lax.rem(s + n_slab - step, n_slab)
        remote("slab", step, send2.at[0], recv2.at[src], c2_s, c2_r).wait_recv()
    lines = split(recv2[...].reshape(n_slab * 2 * rows, L))
    half = 2 * n_slab
    for jj in range(2):
        vbuf[jj * half : (jj + 1) * half] = dot3(lines, table(5 + jj)).reshape(half, rows, L)
    by_low = (tab[6][:, : 2 * half], tab[7][:, : 2 * half])
    for y in range(rows):
        out[0, :, y, :] = acc[y] + dot3(by_low, split(vbuf[:, y, :]))

    for step in map_order:
        meta_copy(step).wait_send()
        data_copy(step).wait_send()
        score_copy(step).wait_send()
    for step in dom_order:
        scatter_copy(step).wait_send()
        gather_copy(step).wait_send()
    for step in slab_order:
        first_copy(step).wait_send()
        spread_copy(step).wait_send()
        second_copy(step).wait_send()


def solution(mesh):
    n_dom, n_map, n_slab = (mesh.shape[a] for a in ("dom", "map", "slab"))
    rows, chunk = L // n_slab, L // n_dom
    tab = tables(n_slab)
    vmem = pl.BlockSpec(memory_space=pltpu.VMEM)
    smem = pl.BlockSpec(memory_space=pltpu.SMEM)
    dma = pltpu.SemaphoreType.DMA

    def local(particles, class_list, orient, ctf_index, tomo_id, defocus, tomo_gain, maps):
        real_grad, scores = pl.pallas_call(
            functools.partial(kernel, (n_dom, n_map, n_slab)),
            out_shape=(
                jax.ShapeDtypeStruct((1, L, rows, L), F32),
                jax.ShapeDtypeStruct((K, P_DEV), F32),
            ),
            in_specs=[vmem] + [smem] * 6 + [vmem] * 2,
            out_specs=(vmem, vmem),
            scratch_shapes=[
                pltpu.VMEM((BOX // 2, 8, L), F32),
                pltpu.VMEM((P_DEV, L, L), F32),
                pltpu.VMEM((n_map, 2 * L, L), BF16),
                pltpu.VMEM((n_map, 2 * L, L), BF16),
                pltpu.VMEM((n_map, 8, L), F32),
                pltpu.VMEM((n_map, 8, L), F32),
                pltpu.VMEM((L, 2 * PLANES, L), F32),
                pltpu.VMEM((rows, 2 * PLANES * n_slab, L), F32),
                pltpu.VMEM((rows, L, L), F32),
                pltpu.VMEM((4, L, L), F32),
                pltpu.VMEM((n_map, 2, L, L), F32),
                pltpu.VMEM((4, L, L), F32),
                pltpu.VMEM((n_map, 8, L), F32),
                pltpu.VMEM((n_map, 8, L), F32),
                pltpu.VMEM((n_map, L), F32),
                pltpu.VMEM((n_slab, n_map, L), F32),
                pltpu.VMEM((L, L), F32),
                pltpu.VMEM((n_dom, chunk, L), F32),
                pltpu.VMEM((chunk, L), F32),
                pltpu.VMEM((L, L), F32),
                pltpu.VMEM((n_slab, 2, rows, L), F32),
                pltpu.VMEM((n_slab, 2, rows, L), F32),
                pltpu.VMEM((4 * n_slab, rows, L), F32),
            ]
            + [dma((n_map,))] * 4
            + [dma((n_slab,))] * 2
            + [dma((n_map,))] * 2
            + [dma((n_slab,))] * 2
            + [dma((n_dom,))] * 4
            + [dma((n_slab,))] * 2,
            compiler_params=pltpu.CompilerParams(
                collective_id=0, has_side_effects=True, vmem_limit_bytes=48 * 2**20
            ),
        )(particles, class_list.T, orient.T, ctf_index, tomo_id, defocus, tomo_gain, maps, tab)
        return real_grad, scores.T

    pair = P(("dom", "map"))
    return jax.shard_map(
        local,
        mesh=mesh,
        in_specs=(
            P(("dom", "map"), "slab", None),
            pair,
            pair,
            pair,
            pair,
            P(),
            P(),
            P("map", "slab", None, None),
        ),
        out_specs=(P("map", None, "slab", None), pair),
        check_vma=False,
    )
```

```python
import functools
import math

import jax
import jax.numpy as jnp
import numpy as np
from jax import lax
from jax.experimental import pallas as pl
from jax.experimental.pallas import tpu as pltpu
from jax.sharding import PartitionSpec as P

L = 128
BOX = 64
K = 2
P_DEV = 4
PLANES = 4
TAU_REG = 0.1
PHASE_SHIFT = 0.1
F32 = jnp.float32
BF16 = jnp.bfloat16
VMEM_BYTES = 63 * 2**20


def wrap(index, size):
    return jnp.where(index < size // 2, index, index - size)


def fast_sin(x):
    turns = jnp.floor(x * (1.0 / math.pi) + 0.5)
    r = x - turns * 3.140625
    r = r - turns * 9.67653589793e-4
    odd = turns - 2.0 * jnp.floor(turns * 0.5)
    r = r * (1.0 - 2.0 * odd)
    s = r * r
    poly = -1.0 / 39916800.0
    for c in (1.0 / 362880.0, -1.0 / 5040.0, 1.0 / 120.0, -1.0 / 6.0):
        poly = poly * s + c
    return r + r * s * poly


def split(x):
    high = x.astype(BF16)
    return high, (x - high.astype(F32)).astype(BF16)


def dot(a, b):
    return jnp.dot(a, b, preferred_element_type=F32)


def dot3(a, b):
    return dot(a[0], b[0]) + (dot(a[0], b[1]) + dot(a[1], b[0]))


def tables(n_slab):
    def cas(rows, cols):
        angle = (np.outer(rows, cols) % L) * (2.0 * math.pi / L)
        return (np.cos(angle) + np.sin(angle)) / math.sqrt(L)

    points = np.arange(L)
    wrapped = np.where(np.arange(BOX) < BOX // 2, np.arange(BOX), np.arange(BOX) - BOX)
    rows = cas(points, points)
    window = cas(wrapped, points)
    q = np.arange(2 * PLANES * n_slab)
    s, r = q // (2 * PLANES), q % (2 * PLANES)
    low = s * PLANES + r
    low = np.where(low < BOX // 2, low, low - BOX)
    freq = np.where(r < PLANES, low, BOX // 2 + s * PLANES + r - PLANES)
    planes = cas(points, freq)
    full = np.zeros((L, L))
    full[:, : len(q)] = planes
    picked = np.zeros((L, L))
    half = 2 * n_slab
    for jj in range(2):
        for row in range(half):
            picked[:, jj * half + row] = planes[:, (row // 2) * 2 * PLANES + 2 * (row % 2) + jj]
    none = np.zeros((BOX, L))
    negate = np.zeros((L, L))
    for block in range(2):
        for a in range(BOX):
            negate[block * BOX + a, block * BOX + (-a) % BOX] = 1.0
    first = np.concatenate([window.T, window.T], axis=1) / 64.0
    mats = [
        rows * TAU_REG,
        rows,
        full,
        picked,
        first,
        np.concatenate([window, none]),
        np.concatenate([none, window]),
        negate,
    ]
    pairs = []
    for mat in mats:
        mat = mat.astype(np.float32)
        high = mat.astype(jnp.bfloat16)
        pairs += [high, (mat - high.astype(np.float32)).astype(jnp.bfloat16)]
    return np.stack(pairs)


def kernel(
    sizes,
    part_hbm,
    cls_hbm,
    ori_hbm,
    cidx_hbm,
    tid_hbm,
    focus_hbm,
    gain_hbm,
    maps_hbm,
    tab_hbm,
    out,
    score_out,
    part,
    cls,
    ori,
    cidx,
    tid,
    focus,
    gain,
    maps,
    tab,
    tmp,
    xs,
    send_z,
    recv_z,
    send_y,
    recv_y,
    send_m,
    meta_z,
    meta_y,
    send1,
    recv1,
    acc,
    wrot,
    wtop,
    wz,
    wy,
    ctf,
    sums,
    scz_send,
    scz_recv,
    scy_send,
    scy_recv,
    ss_send,
    ss_recv,
    dlow,
    dhigh,
    rs_low,
    rs_high,
    red,
    dfull,
    send2,
    recv2,
    vbuf,
    in_sem,
    map_s,
    map_r,
    dom_s,
    dom_r,
    slab_s,
    slab_r,
):
    n_dom, n_map, n_slab = sizes
    n = n_map
    rows = L // n_slab
    chunk = BOX // n_dom
    d, m, s = lax.axis_index("dom"), lax.axis_index("map"), lax.axis_index("slab")

    def remote(to, src, dst, ssem, rsem):
        return pltpu.make_async_remote_copy(
            src_ref=src,
            dst_ref=dst,
            send_sem=ssem,
            recv_sem=rsem,
            device_id=to,
            device_id_type=pl.DeviceIdType.MESH,
        )

    loads = [
        pltpu.make_async_copy(here, there, in_sem.at[i])
        for i, (here, there) in enumerate(
            [
                (part_hbm, part),
                (cls_hbm, cls),
                (ori_hbm, ori),
                (cidx_hbm, cidx),
                (tid_hbm, tid),
                (focus_hbm, focus),
                (gain_hbm, gain),
                (maps_hbm, maps),
                (tab_hbm, tab),
            ]
        )
    ]
    for load in loads[:7]:
        load.start()

    barrier = pltpu.get_barrier_semaphore()

    def greet(to):
        pl.semaphore_signal(barrier, inc=1, device_id=to, device_id_type=pl.DeviceIdType.MESH)

    for step in range(1, n):
        greet({"map": lax.rem(m + step, n)})
        greet({"dom": lax.rem(d + step, n)})
    for step in range(n):

        @pl.when(jnp.logical_or(d != m, step != m))
        def _():
            greet({"dom": m, "map": jnp.int32(step)})

    for step in range(1, n_slab):
        greet({"slab": lax.rem(s + step, n_slab)})
    for load in loads[7:]:
        load.start()

    lane = lax.broadcasted_iota(jnp.int32, (L, L), 1)
    row = lax.broadcasted_iota(jnp.int32, (L, L), 0)
    lane8 = lax.broadcasted_iota(jnp.int32, (8, L), 1)
    row8 = lax.broadcasted_iota(jnp.int32, (8, L), 0)

    loads[0].wait()
    for g in range(2):
        both = jnp.concatenate([part[2 * g].astype(F32), part[2 * g + 1].astype(F32)], axis=0)
        up = pltpu.roll(both, 7, 0)
        for k in range(BOX // 2):
            here, above = both[:, k * L : (k + 1) * L], up[:, k * L : (k + 1) * L]
            even = jnp.where(lane8 < BOX, here, pltpu.roll(above, BOX, 1))
            odd = jnp.where(lane8 < BOX, pltpu.roll(here, BOX, 1), above)
            tmp[k] = jnp.where(row8 % 2 == 0, even, pltpu.roll(odd, 1, 0))
        for i in range(4):
            for h in range(2):
                start = (i % 2) * BOX + h
                xs[2 * g + i // 2, pl.ds(start, BOX // 2, stride=2), :] = tmp[:, 2 * i + h, :]
    for load in loads[1:7]:
        load.wait()

    META, DATA, SCORE, SUM, ALL, WIN = (i * n for i in range(6))

    def meta_copy(axis, c):
        to, there, ssem, rsem = ({"map": c}, meta_z.at[m], map_s, map_r) if axis == "map" else ({"dom": c}, meta_y.at[d], dom_s, dom_r)
        me = m if axis == "map" else d
        return remote(to, send_m.at[c], there, ssem.at[META + c], rsem.at[META + me])

    def data_copy(axis, c):
        if axis == "map":
            return remote({"map": c}, send_z.at[c], recv_z.at[m], map_s.at[DATA + c], map_r.at[DATA + m])
        return remote({"dom": c}, send_y.at[c], recv_y.at[d], dom_s.at[DATA + c], dom_r.at[DATA + d])

    def build(c, carry):
        found = jnp.int32(0)
        who = [jnp.int32(0)] * 2
        turn = [jnp.int32(0)] * 2
        for p in range(P_DEV):
            for j in range(K):
                hit = cls[j, p] == c
                for k in range(2):
                    mine = jnp.logical_and(hit, found == k)
                    who[k] = jnp.where(mine, p, who[k])
                    turn[k] = jnp.where(mine, ori[j, p], turn[k])
                found = found + hit.astype(jnp.int32)
        meta = jnp.zeros((8, L), F32)
        for k in range(2):
            power = jnp.where(found > k, gain[tid[who[k]]], 0.0)
            meta = jnp.where(row8 == 4 * k, focus[cidx[who[k]]], meta)
            meta = jnp.where(row8 == 4 * k + 1, power, meta)
            meta = jnp.where(row8 == 4 * k + 2, turn[k].astype(F32), meta)
            send_z[c, k * BOX : (k + 1) * BOX, :] = xs[who[k], :BOX].astype(BF16)
            send_y[c, k * BOX : (k + 1) * BOX, :] = xs[who[k], BOX:].astype(BF16)
        send_m[c] = meta
        return carry

    lax.fori_loop(0, n, build, 0)

    ahead_m = [lax.rem(m + step, n) for step in range(n)]
    ahead_d = [lax.rem(d + step, n) for step in range(n)]
    ahead_s = [lax.rem(s + step, n_slab) for step in range(n_slab)]
    order = [o for step in range(1, n // 2 + 1) for o in ([step] if 2 * step == n else [step, n - step])]

    def each_map(act):
        for step in order:
            act(ahead_m[step])

    def each_dom(act):
        for step in order:
            act(ahead_d[step])

    def each_slab(act):
        for t in ahead_s[1:]:
            act(t)

    others = (n_dom - 1) + (n_map - 1) + (n_slab - 1)
    pl.semaphore_wait(barrier, others + n - (d == m).astype(jnp.int32))

    for step in order[::-1]:
        data_copy("map", ahead_m[step]).start()
        data_copy("dom", ahead_d[step]).start()
    each_map(lambda c: meta_copy("map", c).start())
    each_dom(lambda c: meta_copy("dom", c).start())

    loads[7].wait()
    lane64 = lane[:BOX]
    halves = []
    for jp in range(2):
        cut = []
        for jj in range(2):
            plane = maps[0, 2 * jp + jj]
            cut.append(jnp.concatenate([plane[: BOX // 2], plane[L - BOX // 2 :]], axis=0))
        first = jnp.where(lane64 < BOX // 2, cut[0], pltpu.roll(cut[0], BOX, 1))
        second = jnp.where(lane64 < L - BOX // 2, pltpu.roll(cut[1], BOX, 1), cut[1])
        halves.append(jnp.where(lane64 < BOX, first, second))
    wtop[0] = halves[0]
    wtop[1] = halves[1]

    def piece_copy(c):
        return remote(
            {"map": c},
            wtop.at[1, pl.ds(pl.multiple_of(d * chunk, chunk), chunk)],
            wz.at[m],
            map_s.at[WIN + c],
            map_r.at[WIN + m],
        )

    each_map(lambda c: piece_copy(c).start())
    wz[m] = wtop[1, pl.ds(pl.multiple_of(d * chunk, chunk), chunk)]

    loads[8].wait()

    def table(i):
        return tab[2 * i], tab[2 * i + 1]

    for q in range(2 * PLANES):
        across = dot3(split(maps[0, q]), table(0))
        send1[:, q, :] = dot3(table(1), split(across))

    FIRST, SPREAD, SECOND = (i * n_slab for i in range(3))

    def first_copy(t):
        return remote(
            {"slab": t},
            send1.at[pl.ds(t * rows, rows)],
            recv1.at[:, pl.ds(pl.multiple_of(s * 2 * PLANES, 2 * PLANES), 2 * PLANES), :],
            slab_s.at[FIRST + t],
            slab_r.at[FIRST + s],
        )

    each_slab(lambda t: first_copy(t).start())
    recv1[:, pl.ds(pl.multiple_of(s * 2 * PLANES, 2 * PLANES), 2 * PLANES), :] = send1[pl.ds(s * rows, rows)]

    def window_copy(c):
        return remote(
            {"dom": c},
            wz.at[c],
            wy.at[pl.ds(pl.multiple_of(d * chunk, chunk), chunk)],
            dom_s.at[WIN + c],
            dom_r.at[WIN + d],
        )

    each_map(lambda c: remote({"map": c}, wz.at[c], wz.at[c], map_s.at[WIN + c], map_r.at[WIN + c]).wait_recv())
    each_dom(lambda c: window_copy(c).start())
    wy[pl.ds(pl.multiple_of(d * chunk, chunk), chunk)] = wz[d]

    fj = wrap(s * PLANES + 2 * (row // BOX) + lane // BOX, BOX)
    fa, fb = wrap(row % BOX, BOX), wrap(lane % BOX, BOX)
    squares = (fj * fj + fa * fa + fb * fb).astype(F32) * (1.0 / (BOX * BOX))

    def contrast(from_z, from_y, slot, total):
        for k in range(2):
            value = from_z[4 * k + 1 : 4 * k + 2] * fast_sin(from_z[4 * k : 4 * k + 1] * squares + PHASE_SHIFT)
            other = from_y[4 * k + 1 : 4 * k + 2] * fast_sin(from_y[4 * k : 4 * k + 1] * squares[BOX:] + PHASE_SHIFT)
            ctf[slot, k, :BOX] = value[:BOX]
            ctf[slot, k, BOX:] = other
            total = total + value * value
        return total

    power = contrast(send_m[m], send_m[d], 0, jnp.zeros((L, L), F32))

    def other_contrast(step, total):
        i, j = lax.rem(m + step, n), lax.rem(d + step, n)
        return contrast(meta_z[i], meta_y[j], step, total)

    each_map(lambda i: remote({"map": i}, send_m.at[i], meta_z.at[i], map_s.at[META + i], map_r.at[META + i]).wait_recv())
    each_dom(lambda j: remote({"dom": j}, send_m.at[j], meta_y.at[j], dom_s.at[META + j], dom_r.at[META + j]).wait_recv())
    power = lax.fori_loop(1, n, other_contrast, power)

    negate = tab[14]

    def by_left(x):
        high, lower = split(x)
        return dot(negate, high) + dot(negate, lower)

    def by_right(x):
        high, lower = split(x)
        return dot(high, negate) + dot(lower, negate)

    def swapped(x):
        t = x.T
        other = pltpu.roll(pltpu.roll(t, BOX, 0), BOX, 1)
        return jnp.where(row // BOX == lane // BOX, t, other)

    for jp in range(2):
        dlow[jp] = wtop[jp] * power[jp * BOX : (jp + 1) * BOX]

    sums[...] = jnp.zeros_like(sums)

    def collect(data, meta, slot, base):
        at = slice(base, base + BOX)
        for k in range(2):
            z = data[k * BOX : (k + 1) * BOX].astype(F32) * ctf[slot, k, at]
            turn = meta[4 * k + 2 : 4 * k + 3]
            for o in range(4):
                sums[o, at] += jnp.where(turn == float(o), z, 0.0)

    collect(send_z[m], send_m[m], 0, 0)
    collect(send_y[d], send_m[d], 0, BOX)

    for step in order:
        p, q = ahead_m[step], ahead_d[step]
        remote({"map": p}, send_z.at[p], recv_z.at[p], map_s.at[DATA + p], map_r.at[DATA + p]).wait_recv()
        collect(recv_z[p], meta_z[p], step, 0)
        remote({"dom": q}, send_y.at[q], recv_y.at[q], dom_s.at[DATA + q], dom_r.at[DATA + q]).wait_recv()
        collect(recv_y[q], meta_y[q], step, BOX)

    turned = swapped(by_left(sums[1]) + by_right(sums[3]))
    turned = turned + sums[0] + by_left(by_right(sums[2]))
    dlow[0] = dlow[0] - turned[:BOX]
    dhigh[...] = -turned[BOX:]

    def low_copy(c):
        return remote(
            {"dom": c},
            dlow.at[:, pl.ds(pl.multiple_of(c * chunk, chunk), chunk), :],
            rs_low.at[d],
            dom_s.at[SUM + c],
            dom_r.at[SUM + d],
        )

    def high_copy(c):
        return remote(
            {"dom": c, "map": d},
            dhigh.at[pl.ds(pl.multiple_of(c * chunk, chunk), chunk)],
            rs_high.at[m],
            map_s.at[SUM + c],
            map_r.at[SUM + m],
        )

    def unless_self(step, act):
        if step == 0:
            pl.when(d != m)(act)
        else:
            act()

    for step in range(n):
        c = lax.rem(d + step, n)
        if step:
            low_copy(c).start()
        unless_self(step, lambda c=c: high_copy(c).start())
    rs_low[d] = dlow[:, pl.ds(pl.multiple_of(d * chunk, chunk), chunk), :]

    @pl.when(d == m)
    def _():
        rs_high[m] = dhigh[pl.ds(pl.multiple_of(d * chunk, chunk), chunk)]

    def wait_window(c):
        piece = wy.at[pl.ds(pl.multiple_of(c * chunk, chunk), chunk)]
        remote({"dom": c}, piece, piece, dom_s.at[WIN + c], dom_r.at[WIN + c]).wait_recv()

    each_dom(wait_window)
    window = jnp.concatenate([wtop[0], wy[...]], axis=0)
    window_n = by_right(window)
    wrot[0] = window
    wrot[1] = swapped(window_n)
    wrot[2] = by_left(window_n)
    wrot[3] = swapped(by_left(window))

    def correlate(data, meta, slot, base):
        lines = jnp.zeros((8, L), F32)
        at = slice(base, base + BOX)
        for k in range(2):
            turn = meta[4 * k + 2 : 4 * k + 3]
            chosen = wrot[3, at]
            for o in (2, 1, 0):
                chosen = jnp.where(turn == float(o), wrot[o, at], chosen)
            found = data[k * BOX : (k + 1) * BOX].astype(F32) * ctf[slot, k, at] * chosen
            lines = jnp.where(row8 == k, jnp.sum(found, axis=0, keepdims=True), lines)
        return lines * (1.0 / BOX**1.5)

    scz_recv[m] = correlate(send_z[m], send_m[m], 0, 0)
    scy_recv[d] = correlate(send_y[d], send_m[d], 0, BOX)

    def score(step, carry):
        p, q = lax.rem(m + step, n), lax.rem(d + step, n)
        scz_send[p] = correlate(recv_z[p], meta_z[p], step, 0)
        scy_send[q] = correlate(recv_y[q], meta_y[q], step, BOX)
        return carry

    lax.fori_loop(1, n, score, 0)

    def score_copies(step):
        p, q = lax.rem(m + step, n), lax.rem(d + step, n)
        return [
            remote({"map": p}, scz_send.at[p], scz_recv.at[m], map_s.at[SCORE + p], map_r.at[SCORE + m]),
            remote({"dom": q}, scy_send.at[q], scy_recv.at[d], dom_s.at[SCORE + q], dom_r.at[SCORE + d]),
        ]

    for step in range(1, n):
        for copy in score_copies(step):
            copy.start()

    for step in range(1, n):
        c = lax.rem(d + step, n)
        remote({"dom": c}, rs_low.at[c], rs_low.at[c], dom_s.at[SUM + c], dom_r.at[SUM + c]).wait_recv()
    for c in range(n):

        @pl.when(jnp.logical_or(d != m, c != m))
        def _():
            piece = rs_high.at[c]
            remote({"dom": m, "map": jnp.int32(c)}, piece, piece, map_s.at[SUM + c], map_r.at[SUM + c]).wait_recv()

    total = rs_low[0]
    high = rs_high[0]
    for i in range(1, n):
        total = total + rs_low[i]
        high = high + rs_high[i]
    red[0] = total[0]
    red[1] = total[1] + high

    def all_copy(c):
        return remote(
            {"dom": c},
            red,
            dfull.at[:, pl.ds(pl.multiple_of(d * chunk, chunk), chunk), :],
            dom_s.at[ALL + c],
            dom_r.at[ALL + d],
        )

    for step in range(1, n):
        all_copy(lax.rem(d + step, n)).start()
    dfull[:, pl.ds(pl.multiple_of(d * chunk, chunk), chunk), :] = red[...]

    for step in range(1, n):
        p, q = lax.rem(m + step, n), lax.rem(d + step, n)
        remote({"map": p}, scz_send.at[p], scz_recv.at[p], map_s.at[SCORE + p], map_r.at[SCORE + p]).wait_recv()
        remote({"dom": q}, scy_send.at[q], scy_recv.at[q], dom_s.at[SCORE + q], dom_r.at[SCORE + q]).wait_recv()
    flat = [jnp.sum(scz_recv[:, k, :] + scy_recv[:, k, :], axis=1, keepdims=True) for k in range(2)]
    lane_m = lax.broadcasted_iota(jnp.int32, (n_map, L), 1)
    ss_send[...] = jnp.where(lane_m == 0, flat[0], jnp.where(lane_m == 1, flat[1], 0.0))

    def spread_copy(t):
        return remote({"slab": t}, ss_send, ss_recv.at[s], slab_s.at[SPREAD + t], slab_r.at[SPREAD + s])

    each_slab(lambda t: spread_copy(t).start())
    ss_recv[s] = ss_send[...]

    for step in range(1, n):
        c = lax.rem(d + step, n)
        piece = dfull.at[:, pl.ds(pl.multiple_of(c * chunk, chunk), chunk), :]
        remote({"dom": c}, red, piece, dom_s.at[ALL + c], dom_r.at[ALL + c]).wait_recv()

    for jp in range(2):
        columns = dot3(
            (tab[8][:, :BOX], tab[9][:, :BOX]), split(dfull[jp])
        )
        send2[:, jp] = columns.reshape(n_slab, rows, L)

    def second_copy(t):
        return remote({"slab": t}, send2.at[t], recv2.at[s], slab_s.at[SECOND + t], slab_r.at[SECOND + s])

    each_slab(lambda t: second_copy(t).start())
    recv2[s] = send2[s]

    def wait_first(t):
        there = recv1.at[:, pl.ds(pl.multiple_of(t * 2 * PLANES, 2 * PLANES), 2 * PLANES), :]
        remote({"slab": t}, send1.at[pl.ds(t * rows, rows)], there, slab_s.at[FIRST + t], slab_r.at[FIRST + t]).wait_recv()

    each_slab(wait_first)
    deep = 2 * PLANES * n_slab
    by_plane = (tab[4][:, :deep], tab[5][:, :deep])
    for y in range(rows):
        acc[y] = dot3(by_plane, split(recv1[y]))

    def sent_map(c):
        meta_copy("map", c).wait_send()
        data_copy("map", c).wait_send()
        piece_copy(c).wait_send()

    def sent_dom(c):
        meta_copy("dom", c).wait_send()
        data_copy("dom", c).wait_send()
        window_copy(c).wait_send()
        low_copy(c).wait_send()
        all_copy(c).wait_send()

    def sent_slab(t):
        first_copy(t).wait_send()
        spread_copy(t).wait_send()

    each_map(sent_map)
    each_dom(sent_dom)
    each_slab(sent_slab)
    for step in range(n):
        c = lax.rem(d + step, n)
        unless_self(step, lambda c=c: high_copy(c).wait_send())
        if step:
            for copy in score_copies(step):
                copy.wait_send()

    each_slab(
        lambda t: remote({"slab": t}, ss_send, ss_recv.at[t], slab_s.at[SPREAD + t], slab_r.at[SPREAD + t]).wait_recv()
    )
    tally = ss_recv[0]
    for i in range(1, n_slab):
        tally = tally + ss_recv[i]
    row_m = lax.broadcasted_iota(jnp.int32, (n_map, L), 0)
    out_row = lax.broadcasted_iota(jnp.int32, (K, P_DEV), 0)
    out_col = lax.broadcasted_iota(jnp.int32, (K, P_DEV), 1)
    found = jnp.zeros((K, P_DEV), F32)
    for p in range(P_DEV):
        for i in range(K):
            c = cls[i, p]
            rank = jnp.int32(0)
            for e in range(p * K + i):
                rank = rank + (cls[e % K, e // K] == c).astype(jnp.int32)
            here = jnp.logical_and(row_m == c, lane_m == rank)
            one = jnp.sum(jnp.where(here, tally, 0.0), axis=0, keepdims=True)
            one = jnp.sum(one, axis=1, keepdims=True)
            found = jnp.where(jnp.logical_and(out_row == i, out_col == p), one, found)
    score_out[...] = found

    each_slab(
        lambda t: remote({"slab": t}, send2.at[t], recv2.at[t], slab_s.at[SECOND + t], slab_r.at[SECOND + t]).wait_recv()
    )
    lines = split(recv2[...].reshape(n_slab * 2 * rows, L))
    half = 2 * n_slab
    for jj in range(2):
        vbuf[jj * half : (jj + 1) * half] = dot3(lines, table(5 + jj)).reshape(half, rows, L)
    by_low = (tab[6][:, : 2 * half], tab[7][:, : 2 * half])
    for y in range(rows):
        out[0, :, y, :] = acc[y] + dot3(by_low, split(vbuf[:, y, :]))

    each_slab(lambda t: second_copy(t).wait_send())


def solution(mesh):
    n_dom, n_map, n_slab = (mesh.shape[a] for a in ("dom", "map", "slab"))
    rows, chunk = L // n_slab, BOX // n_dom
    tab = tables(n_slab)
    vmem = pl.BlockSpec(memory_space=pltpu.VMEM)
    hbm = pl.BlockSpec(memory_space=pltpu.HBM)
    dma = pltpu.SemaphoreType.DMA

    def local(particles, class_list, orient, ctf_index, tomo_id, defocus, tomo_gain, maps):
        args = (particles, class_list.T, orient.T, ctf_index, tomo_id, defocus, tomo_gain, maps, tab)
        spaces = [pltpu.VMEM] + [pltpu.SMEM] * 6 + [pltpu.VMEM] * 2
        real_grad, scores = pl.pallas_call(
            functools.partial(kernel, (n_dom, n_map, n_slab)),
            out_shape=(
                jax.ShapeDtypeStruct((1, L, rows, L), F32),
                jax.ShapeDtypeStruct((K, P_DEV), F32),
            ),
            in_specs=[hbm] * len(args),
            out_specs=(vmem, vmem),
            scratch_shapes=[space(arg.shape, arg.dtype) for space, arg in zip(spaces, args)]
            + [
                pltpu.VMEM((BOX // 2, 8, L), F32),
                pltpu.VMEM((P_DEV, L, L), F32),
            ]
            + [pltpu.VMEM((n_map, L, L), BF16)] * 4
            + [pltpu.VMEM((n_map, 8, L), F32)] * 3
            + [
                pltpu.VMEM((L, 2 * PLANES, L), F32),
                pltpu.VMEM((rows, 2 * PLANES * n_slab, L), F32),
                pltpu.VMEM((rows, L, L), F32),
                pltpu.VMEM((4, L, L), F32),
                pltpu.VMEM((2, BOX, L), F32),
                pltpu.VMEM((n_map, chunk, L), F32),
                pltpu.VMEM((BOX, L), F32),
                pltpu.VMEM((n_map, 2, L, L), F32),
                pltpu.VMEM((4, L, L), F32),
            ]
            + [pltpu.VMEM((n_map, 8, L), F32)] * 4
            + [
                pltpu.VMEM((n_map, L), F32),
                pltpu.VMEM((n_slab, n_map, L), F32),
                pltpu.VMEM((2, BOX, L), F32),
                pltpu.VMEM((BOX, L), F32),
                pltpu.VMEM((n_dom, 2, chunk, L), F32),
                pltpu.VMEM((n_map, chunk, L), F32),
                pltpu.VMEM((2, chunk, L), F32),
                pltpu.VMEM((2, BOX, L), F32),
                pltpu.VMEM((n_slab, 2, rows, L), F32),
                pltpu.VMEM((n_slab, 2, rows, L), F32),
                pltpu.VMEM((4 * n_slab, rows, L), F32),
                dma((len(args),)),
            ]
            + [dma((6 * n_map,))] * 4
            + [dma((3 * n_slab,))] * 2,
            compiler_params=pltpu.CompilerParams(
                collective_id=0, has_side_effects=True, vmem_limit_bytes=VMEM_BYTES
            ),
        )(*args)
        return real_grad, scores.T

    pair = P(("dom", "map"))
    return jax.shard_map(
        local,
        mesh=mesh,
        in_specs=(
            P(("dom", "map"), "slab", None),
            pair,
            pair,
            pair,
            pair,
            P(),
            P(),
            P("map", "slab", None, None),
        ),
        out_specs=(P("map", None, "slab", None), pair),
        check_vma=False,
    )
```
